32 devices in a mesh: tile: 8 (over y, x, core), layer: 4 (over z).
Axes of the slice: x: 2, y: 2, z: 4, core: 2. Of those that a mesh axis runs over, the one named last changes fastest.
Arguments:
- permeability: float32 [3, 128, 16, 256], P(None, 'tile', 'layer'), may hold values from 0.05 to 20
- porosity: float32 [128, 16, 256], P('tile', 'layer'), may hold values from 0.1 to 0.3
- saturation: float32 [128, 16, 256], P('tile', 'layer'), may hold values from 0.15 to 0.85
- pressure_old: float32 [128, 16, 256], P('tile', 'layer'), may hold values from -6 to 6
- source: float32 [128, 16, 256], P('tile', 'layer'), may hold values from -6 to 6
Outputs:
- pressure: float32 [128, 16, 256], P('tile', 'layer')
- water_sat: float32 [128, 16, 256], P('tile', 'layer')
The draws below stay inside these ranges and needn't reach their ends.
All inputs are finite; a program needn't handle non-finite values.
Results may differ from the reference program's by a relative error of at most 0.0003.
Values sent between devices are 32-bit elements; how exact they have to be, the bound alone decides.
No kernel may reach another device: no remote copies, remote signals or barrier semaphores. Data moves between devices by JAX's collectives and lax.ppermute only.
A program may use at most 128 MiB of HBM per device.

```python
import math
import jax
import jax.numpy as jnp

NY = 256
LEVELS = 3
SWEEPS = 2
COARSE_SWEEPS = 4
CYCLES = 2
SUBSTEPS = 4
NX = 128
NZ = 16


def draw_source(key, part):
    key = jax.random.fold_in(key, 7)
    rough = jax.random.normal(key, (NX, NZ, NY), jnp.float32)
    return jnp.clip(rough, -6.0, 6.0)


def level_of(stream_key, shape, split, low, top_value):
    def one(dim, shards_of):
        draws = jax.random.uniform(jax.random.fold_in(jax.random.fold_in(stream_key, 6), dim), (shards_of,), jnp.float32, low / len(split), top_value / len(split))
        return jnp.repeat(jnp.exp(draws), shape[dim] // shards_of).reshape((-1,) + (1,) * (len(shape) - dim - 1))

    gain = one(*split[0])
    for cut in split[1:]:
        gain = gain * one(*cut)
    return gain


def bell_draw(key, dims, deviation, limit, shards=(), held_as=jnp.bfloat16):
    gain = level_of(key, dims, shards, -0.22, 0.18) if shards else 1.0
    values = jax.random.normal(key, dims, jnp.float32) * deviation * gain
    return jnp.minimum(jnp.maximum(values, -limit), limit).astype(held_as)


def setup_inputs(seed: int = 0) -> dict:
    key_list = jax.random.split(jax.random.key(seed), 6)
    return {
        "permeability": jnp.clip(jnp.exp(math.log(20.0) - 5.9914645 * jax.random.uniform(key_list[0], (3, NX, NZ, NY), jnp.float32) ** level_of(key_list[0], (3, NX, NZ, NY), ((1, 8), (2, 4)), -0.2, 0.2)), 0.05, 20.0),
        "porosity": jnp.clip(0.1 + 0.20000001043081284 * jax.random.uniform(key_list[1], (NX, NZ, NY), jnp.float32) ** level_of(key_list[1], (NX, NZ, NY), ((0, 8), (1, 4)), -0.2, 0.2), 0.1, 0.3),
        "saturation": jnp.clip(0.15 + 0.70000002 * jax.random.uniform(key_list[2], (NX, NZ, NY), jnp.float32) ** level_of(key_list[2], (NX, NZ, NY), ((0, 8), (1, 4)), -0.2, 0.2), 0.15, 0.85),
        "pressure_old": bell_draw(key_list[3], (NX, NZ, NY), 1.0, 6.0, ((0, 8), (1, 4)), jnp.float32),
        "source": draw_source(jax.random.fold_in(key_list[5], 71), 0),
    }


OMEGA = 0.8
STORE_RATE = 0.02
STEP_RATE = 0.02
OIL_RATIO = 0.25
DIRECTIONS = (0, 0, 2, 2, 1, 1)


def harmonic(left, right):
    return 2.0 * left * right / (left + right)


def neighbours(padded):
    return [padded[:, :-2, 1:-1, 1:-1], padded[:, 2:, 1:-1, 1:-1],
            padded[:, 1:-1, :-2, 1:-1], padded[:, 1:-1, 2:, 1:-1],
            padded[:, 1:-1, 1:-1, :-2], padded[:, 1:-1, 1:-1, 2:]]


def pad_zeros(values):
    return jnp.pad(values, ((0, 0), (1, 1), (1, 1), (1, 1)))


def fraction(water):
    wetting = water * water
    return wetting / (wetting + OIL_RATIO * (1.0 - water) * (1.0 - water))


def restrict(values):
    parts, extent_x, extent_z, extent_y = values.shape
    blocks = values.reshape(parts, extent_x // 2, 2, extent_z // 2, 2, extent_y // 2, 2)
    return blocks.sum(axis=(2, 4, 6))


def prolong(values):
    return jnp.repeat(jnp.repeat(jnp.repeat(values, 2, 1), 2, 2), 2, 3)


def coarsen(coefficients):
    parts, extent_x, extent_z, extent_y = coefficients.shape
    blocks = coefficients.reshape(parts, extent_x // 2, 2, extent_z // 2, 2, extent_y // 2, 2)
    along_x = harmonic(blocks[0:1, :, 0], blocks[0:1, :, 1]).sum(axis=(3, 5))
    along_y = harmonic(blocks[1:2, :, :, :, :, :, 0], blocks[1:2, :, :, :, :, :, 1]).sum(axis=(2, 4))
    along_z = harmonic(blocks[2:3, :, :, :, 0], blocks[2:3, :, :, :, 1]).sum(axis=(2, 5))
    return 0.5 * jnp.concatenate([along_x, along_y, along_z], 0)


def build_level(coefficients, storage):
    beside_all = neighbours(pad_zeros(coefficients))
    face_list = [harmonic(coefficients[comp:comp + 1], beside_all[index][comp:comp + 1])
                 for index, comp in enumerate(DIRECTIONS)]
    diagonal = storage
    for face_value in face_list:
        diagonal = diagonal + face_value
    return storage, face_list, diagonal


def operate(level, iterate):
    storage, face_list, diagonal = level
    beside_all = neighbours(pad_zeros(iterate))
    applied = storage * iterate
    for face_value, other_value in zip(face_list, beside_all):
        applied = applied + face_value * (iterate - other_value)
    return applied


def smooth(level, iterate, right_side):
    return iterate + OMEGA * (right_side - operate(level, iterate)) / level[2]


def cycle(levels, level_index, right_side, iterate):
    level = levels[level_index]
    if level_index == LEVELS - 1:
        for sweep_index in range(COARSE_SWEEPS):
            iterate = smooth(level, iterate, right_side)
        return iterate
    for sweep_index in range(SWEEPS):
        iterate = smooth(level, iterate, right_side)
    residual = right_side - operate(level, iterate)
    restricted = restrict(residual)
    correction = cycle(levels, level_index + 1, restricted, jnp.zeros_like(restricted))
    iterate = iterate + prolong(correction)
    for sweep_index in range(SWEEPS):
        iterate = smooth(level, iterate, right_side)
    return iterate


def reference(permeability, porosity, saturation, pressure_old, source):
    water = saturation[None]
    pores = porosity[None]
    sources = source[None]
    mobility = water * water + OIL_RATIO * (1.0 - water) * (1.0 - water)
    coefficients = permeability * mobility
    storage = STORE_RATE * pores
    levels = []
    for level_index in range(LEVELS):
        if level_index > 0:
            coefficients = coarsen(coefficients)
            storage = restrict(storage)
        levels.append(build_level(coefficients, storage))
    right_side = levels[0][0] * pressure_old[None] + sources
    pressure = pressure_old[None]
    for cycle_index in range(CYCLES):
        pressure = cycle(levels, 0, right_side, pressure)
    beside_all = neighbours(pad_zeros(pressure))
    fluxes = [face_value * (pressure - other_value) for face_value, other_value in zip(levels[0][1], beside_all)]
    inject = jnp.maximum(sources, 0.0)
    produce = jnp.minimum(sources, 0.0)
    for substep in range(SUBSTEPS):
        flowing = fraction(water)
        beside = neighbours(pad_zeros(flowing))
        outflow = jnp.zeros_like(water)
        for flux_value, other_value in zip(fluxes, beside):
            outflow = outflow + flux_value * jnp.where(flux_value > 0.0, flowing, other_value)
        water = water + STEP_RATE / pores * (inject + flowing * produce - outflow)
    return pressure[0], water[0]
```

```python
import functools

import jax
import jax.numpy as jnp
from jax import lax
from jax.experimental import pallas as pl
from jax.experimental.pallas import tpu as pltpu
from jax.sharding import PartitionSpec as P

OMEGA = 0.8
STORE_RATE = 0.02
STEP_RATE = 0.02
OIL_RATIO = 0.25
SUBSTEPS = 4
COARSE_SWEEPS = 4

STRIPS = 4
EDGE = 32
HALO = 6
LANES = 128


def harmonic(left, right):
    return 2.0 * left * right / (left + right)


def lanes_roll(cells, shift):
    return pltpu.roll(cells, shift % cells.shape[1], 1)


def subs_roll(cells, shift):
    return pltpu.roll(cells, shift % cells.shape[0], 0)


def strip_of(layer):
    return layer ^ (layer >> 1)


def lane_ids(rows):
    return lax.broadcasted_iota(jnp.int32, (rows, LANES), 1)


def sub_ids(rows):
    return lax.broadcasted_iota(jnp.int32, (rows, LANES), 0)


def y_open(rows, strip, width):
    lane = lane_ids(rows)
    low = (lane >= EDGE - width) & (lane < EDGE) & (strip == 0)
    high = (lane >= LANES - EDGE - width) & (lane < LANES - EDGE) & (strip == STRIPS - 1)
    return jnp.logical_not(low | high)


def pair_lanes(cells, even, width):
    total = cells + lanes_roll(cells, -width)
    return jnp.where(even, total, lanes_roll(total, width))


def pair_subs(cells, even):
    total = cells + subs_roll(cells, -1)
    return jnp.where(even, total, subs_roll(total, 1))


def neighbour_sum(v, below, above, fx, fx_next, fy, fz, z_width, y_width):
    along_x = fx * below + fx_next * above
    along_z = fz * subs_roll(v, -z_width) + subs_roll(fz * v, z_width)
    along_y = fy * lanes_roll(v, -y_width) + lanes_roll(fy * v, y_width)
    return along_x + along_z + along_y


class Level:
    def __init__(self, fx, fy, fz, w, d, z_width, y_width):
        self.fx, self.fy, self.fz, self.w, self.d = fx, fy, fz, w, d
        self.widths = (z_width, y_width)

    def right_plus(self, i, r, v, below, above):
        return r + neighbour_sum(v, below, above, self.fx(i), self.fx(i + 1), self.fy(i), self.fz(i), *self.widths)

    def sweep(self, ref, right, low, high):
        below, v = ref[low - 1], ref[low]
        for i in range(low, high):
            above = ref[i + 1]
            ref[i] = (1.0 - OMEGA) * v + self.w(i) * self.right_plus(i, right(i), v, below, above)
            below, v = v, above

    def residual(self, ref, right, i):
        v = ref[i]
        return self.right_plus(i, right(i), v, ref[i - 1], ref[i + 1]) - self.d(i) * v


def build(coef, storage, rows, d_rows, fx_s, fy_s, fz_s, w_s, d_s, x_closed, z_open, y_mask, z_width, y_width):
    low, high = rows
    prev = None
    for i in range(low, high):
        cx, cy, cz = coef(0, i), coef(1, i), coef(2, i)
        if prev is not None:
            face = harmonic(prev, cx)
            if i in x_closed:
                face = jnp.where(x_closed[i], 0.0, face)
            fx_s[i] = face
        prev = cx
        fy_s[i] = jnp.where(y_mask, harmonic(cy, lanes_roll(cy, -y_width)), 0.0)
        fz_s[i] = jnp.where(z_open, harmonic(cz, subs_roll(cz, -z_width)), 0.0)
    for i in range(*d_rows):
        fy, fz = fy_s[i], fz_s[i]
        diagonal = storage(i) + fx_s[i] + fx_s[i + 1]
        diagonal = diagonal + fy + lanes_roll(fy, y_width) + fz + subs_roll(fz, z_width)
        d_s[i] = diagonal
        w_s[i] = OMEGA / diagonal


def split_kernel(perm, poro, sat, pres, src, *rest):
    outs, sems = rest[:STRIPS], rest[STRIPS:]
    del sems
    layer = lax.axis_index("layer")
    x, z = poro.shape[0], poro.shape[1]
    lane = lane_ids(z)

    def fill(me):
        target = {strip_of(me ^ j): outs[j] for j in range(STRIPS)}
        for a in range(7):
            for i in range(x):
                row = perm[a, i] if a < 3 else (poro, sat, pres, src)[a - 3][i]
                left, right = row[:, :LANES], row[:, LANES:]
                left_up, left_down = lanes_roll(left, EDGE), lanes_roll(left, -EDGE)
                right_up, right_down = lanes_roll(right, EDGE), lanes_roll(right, -EDGE)
                target[0][a, i] = left_up
                target[1][a, i] = jnp.where(lane < LANES - EDGE, left_down, right_down)
                target[2][a, i] = jnp.where(lane < EDGE, left_up, right_up)
                target[3][a, i] = right_down

    for me in range(STRIPS):
        pl.when(layer == me)(functools.partial(fill, me))


def window_kernel(c0, c1, c2, c3, win, head, tail, coarse, pair_z):
    layer = lax.axis_index("layer")
    chunks = (c0, c1, c2, c3)
    x = c0.shape[1]
    z = STRIPS * c0.shape[2]

    def fill(me):
        order = [chunks[me ^ k] for k in range(STRIPS)]
        for i in range(x):
            def row(a):
                return jnp.concatenate([c[a, i] for c in order], axis=0)

            water = row(4)
            mobility = water * water + OIL_RATIO * (1.0 - water) * (1.0 - water)
            for a in range(7):
                value = water if a == 4 else row(a)
                if a < 3:
                    value = value * mobility
                win[a, i] = value
                if i < HALO:
                    head[pl.ds((a * HALO + i) * z, z), :] = value
                if i >= x - HALO:
                    tail[pl.ds((a * HALO + i - x + HALO) * z, z), :] = value

    for me in range(STRIPS):
        pl.when(layer == me)(functools.partial(fill, me))

    base = 7 * HALO * z
    half = z // 2
    even = lane_ids(half) % 2 == 0

    def put(c, k, value):
        at = (c * (x // 2) + k) * half
        coarse[pl.ds(at, half), :] = value
        head[pl.ds(base + at, half), :] = value
        tail[pl.ds(base + at, half), :] = value

    def pairs(slot, cells):
        pair_z[slot] = cells
        return pair_z[slot, pl.ds(0, half, stride=2), :], pair_z[slot, pl.ds(1, half, stride=2), :]

    for k in range(x // 2):
        along_x = harmonic(win[0, 2 * k], win[0, 2 * k + 1])
        low, high = pairs(4 * k, along_x)
        put(0, k, 0.5 * pair_lanes(low + high, even, 1))
        first, second = win[1, 2 * k], win[1, 2 * k + 1]
        along_y = harmonic(first, lanes_roll(first, -1)) + harmonic(second, lanes_roll(second, -1))
        low, high = pairs(4 * k + 1, along_y)
        total = low + high
        put(1, k, 0.5 * jnp.where(even, total, lanes_roll(total, 1)))
        low, high = pairs(4 * k + 2, win[2, 2 * k])
        along_z = harmonic(low, high)
        low, high = pairs(4 * k + 2, win[2, 2 * k + 1])
        along_z = along_z + harmonic(low, high)
        put(2, k, 0.5 * pair_lanes(along_z, even, 1))
        low, high = pairs(4 * k + 3, STORE_RATE * (win[3, 2 * k] + win[3, 2 * k + 1]))
        put(3, k, pair_lanes(low + high, even, 1))


def restrict_rows(residual, rows, scratch, put):
    for k, i in enumerate(range(rows[0], rows[1], 2)):
        total = residual(i) + residual(i + 1)
        z = total.shape[0]
        scratch[k] = total
        low = scratch[k, pl.ds(0, z // 2, stride=2), :]
        high = scratch[k, pl.ds(1, z // 2, stride=2), :]
        put(k, pair_lanes(low + high, lane_ids(z // 2) % 2 == 0, 1))


def halo_row(win, before, after, a, i, x, z):
    if i < HALO:
        return before[pl.ds((a * HALO + i) * z, z), :]
    if i < HALO + x:
        return win[a, i - HALO]
    return after[pl.ds((a * HALO + i - HALO - x) * z, z), :]


def fine_level(fine, diag):
    x = diag.shape[0]
    return Level(
        lambda i: fine[0, i], lambda i: fine[1, i], lambda i: fine[2, i], lambda i: fine[3, i],
        lambda i: diag[i], 1, 1,
    )


def first_kernel(tiles, win, before, after, fine, diag, iterate, restricted, head, tail, v, pair_z):
    tile, layer = lax.axis_index("tile"), lax.axis_index("layer")
    strip = strip_of(layer)
    x, z = win.shape[1], win.shape[2]
    rows = x + 2 * HALO

    def cells(a, i):
        return halo_row(win, before, after, a, i, x, z)

    build(
        cells, lambda i: STORE_RATE * cells(3, i), (0, rows), (1, rows - 1),
        fine.at[0], fine.at[1], fine.at[2], fine.at[3], fine.at[5],
        {HALO: tile == 0, HALO + x: tile == tiles - 1},
        sub_ids(z) < z - 1, y_open(z, strip, 1), 1, 1,
    )
    for i in range(rows):
        fine[4, i] = STORE_RATE * cells(3, i) * cells(5, i) + cells(6, i)
        v[i] = cells(5, i)
    for i in range(x):
        diag[i] = fine[5, i + HALO]
    level = fine_level(fine, diag)
    level.d = lambda i: diag[i - HALO]
    down(level, fine, v, x, 2, iterate, restricted, head, tail, pair_z)


def down(level, fine, v, x, spare, iterate, restricted, head, tail, pair_z):
    right = lambda i: fine[4, i]
    low, high = HALO, HALO + x
    level.sweep(v, right, low - spare, high + spare)
    level.sweep(v, right, low - spare + 1, high + spare - 1)
    z = v.shape[1]
    half = z // 2

    def put(k, value):
        for ref in (restricted, head, tail):
            if ref is not None:
                ref[pl.ds(k * half, half), :] = value

    restrict_rows(lambda i: level.residual(v, right, i), (low, high), pair_z, put)
    for i in range(x):
        value = v[low + i]
        iterate[i] = value
        if head is not None and i < HALO:
            head[pl.ds(x // 2 * half + i * z, z), :] = value
        if tail is not None and i >= x - HALO:
            tail[pl.ds(x // 2 * half + (i - x + HALO) * z, z), :] = value


def coarse_build(tiles, c_here, c_before, c_after, c_before2, c_after2, base, one, two, x):
    tile, layer = lax.axis_index("tile"), lax.axis_index("layer")
    strip = strip_of(layer)
    count = x // 2
    half = c_here.shape[0] // (4 * count)
    sources = ((c_before2, 0), (c_before, base), (c_here, 0), (c_after, base), (c_after2, 0))

    def cells(c, i):
        ref, start = sources[i // count]
        return ref[pl.ds(start + (c * count + i % count) * half, half), :]

    rows = 5 * count
    own = 2 * count
    build(
        cells, lambda i: cells(3, i), (0, rows), (1, rows - 1),
        one.at[0], one.at[1], one.at[2], one.at[3], one.at[4],
        {own: tile == 0, own - count: tile == 1, own + count: tile == tiles - 1, own + 2 * count: tile == tiles - 2},
        sub_ids(half) < half - 1, y_open(half, strip, 2), 1, 2,
    )
    even_z = sub_ids(half) % 2 == 0
    even_y = lane_ids(half) % 4 < 2

    def cells2(c, k):
        first, second = cells(c, 2 * k), cells(c, 2 * k + 1)
        if c == 0:
            return 0.5 * pair_lanes(pair_subs(harmonic(first, second), even_z), even_y, 2)
        if c == 1:
            total = harmonic(first, lanes_roll(first, -2)) + harmonic(second, lanes_roll(second, -2))
            return 0.5 * pair_subs(jnp.where(even_y, total, lanes_roll(total, 2)), even_z)
        if c == 2:
            total = harmonic(first, subs_roll(first, -1)) + harmonic(second, subs_roll(second, -1))
            return 0.5 * pair_lanes(jnp.where(even_z, total, subs_roll(total, 1)), even_y, 2)
        return pair_lanes(pair_subs(first + second, even_z), even_y, 2)

    rows2, count2 = rows // 2, count // 2
    own2 = 2 * count2
    build(
        cells2, lambda k: cells2(3, k), (0, rows2), (1, rows2 - 1),
        two.at[0], two.at[1], two.at[2], two.at[3], two.at[4],
        {own2: tile == 0, own2 - count2: tile == 1, own2 + count2: tile == tiles - 1, own2 + 2 * count2: tile == tiles - 2},
        sub_ids(half) < half - 2, y_open(half, strip, 4), 2, 4,
    )


def coarse_solve(one, two, right, u, v2, r2, x):
    count = x // 2
    rows = 5 * count
    own = 2 * count
    half = u.shape[1]
    level1 = Level(lambda i: one[0, i], lambda i: one[1, i], lambda i: one[2, i], lambda i: one[3, i], lambda i: one[4, i], 1, 2)
    level2 = Level(lambda i: two[0, i], lambda i: two[1, i], lambda i: two[2, i], lambda i: two[3, i], lambda i: two[4, i], 2, 4)
    need = HALO // 2
    post = need + 2
    need2 = (post + 1) // 2
    wide2 = need2 + COARSE_SWEEPS - 1
    wide = 2 * wide2
    for i in range(own - wide - 2, own + count + wide + 2):
        u[i] = one[3, i] * right(i)
    level1.sweep(u, right, own - wide - 1, own + count + wide + 1)
    even_z = sub_ids(half) % 2 == 0
    even_y = lane_ids(half) % 4 < 2
    own2, count2 = own // 2, count // 2
    for k in range(own2 - wide2, own2 + count2 + wide2):
        total = level1.residual(u, right, 2 * k) + level1.residual(u, right, 2 * k + 1)
        value = pair_lanes(pair_subs(total, even_z), even_y, 2)
        r2[k] = value
        v2[k] = two[3, k] * value
    for step in range(1, COARSE_SWEEPS):
        level2.sweep(v2, lambda k: r2[k], own2 - wide2 + step, own2 + count2 + wide2 - step)
    for i in range(own - post, own + count + post):
        u[i] = u[i] + v2[i // 2]
    level1.sweep(u, right, own - post + 1, own + count + post - 1)
    level1.sweep(u, right, own - need, own + count + need)


def correct(u, v, x, spread, here, before, after):
    count = x // 2
    half = u.shape[1]
    z = 2 * half
    first = 2 * count - HALO // 2
    for k in range(count + HALO):
        value = u[first + k]
        spread[k, pl.ds(0, half, stride=2), :] = value
        spread[k, pl.ds(1, half, stride=2), :] = value
    for i in range(x + 2 * HALO):
        if i < HALO:
            base = before[pl.ds(count * half + i * z, z), :]
        elif i < HALO + x:
            base = here[i - HALO]
        else:
            base = after[pl.ds(count * half + (i - HALO - x) * z, z), :]
        v[i] = base + spread[i // 2]


def right_rows(x, half, here, before, after, before2, after2):
    count = x // 2
    sources = (before2, before, here, after, after2)
    return lambda i: sources[i // count][pl.ds(i % count * half, half), :]


PACK = 8


def second_kernel(tiles, fine, diag, iterate, restricted, before, after, before2, after2, c_here, c_before, c_after, c_before2, c_after2,
                  one, two, iterate_out, message, v, u, v2, r2, spread, pair_z):
    x, z = iterate.shape[0], iterate.shape[1]
    half = z // 2
    coarse_build(tiles, c_here, c_before, c_after, c_before2, c_after2, 7 * HALO * z, one, two, x)
    coarse_solve(one, two, right_rows(x, half, restricted, before, after, before2, after2), u, v2, r2, x)
    correct(u, v, x, spread, iterate, before, after)
    level = fine_level(fine, diag)
    level.d = lambda i: diag[i - HALO]
    right = lambda i: fine[4, i]
    level.sweep(v, right, HALO - 4, HALO + x + 4)
    level.sweep(v, right, HALO - 3, HALO + x + 3)
    down(level, fine, v, x, 2, iterate_out, message, None, None, pair_z)
    for k in range(x // 2):
        at = pl.ds(k * half, half)
        message[at, :] = lanes_roll(message[at, :], LANES // 2)
    lane = lane_ids(z)
    near = LANES - EDGE - PACK
    per = LANES // (2 * PACK)
    packed = None
    for i in range(x):
        value = iterate_out[i]
        value = jnp.where(lane >= near + PACK, lanes_roll(value, LANES // 2), value)
        value = lanes_roll(value, 2 * PACK * (i % per) - near)
        packed = value if i % per == 0 else jnp.where(lane >= 2 * PACK * (i % per), value, packed)
        if i % per == per - 1:
            message[pl.ds(x // 2 * half + i // per * z, z), :] = packed


def widen_kernel(iterate, here, from1, from2, wide, restricted, head, tail):
    layer = lax.axis_index("layer")
    strip = strip_of(layer)
    x, z = iterate.shape[0], iterate.shape[1]
    half = z // 2
    is_even = strip % 2 == 0
    lane = lane_ids(half)
    for k in range(x // 2):
        at = pl.ds(k * half, half)
        first, second = from1[at, :], from2[at, :]
        left = jnp.where(is_even, second, first)
        right = jnp.where(is_even, first, second)
        own = lanes_roll(here[at, :], LANES // 2)
        value = jnp.where(lane < EDGE, left, jnp.where(lane < LANES - EDGE, own, right))
        for ref in (restricted, head, tail):
            ref[at, :] = value
    lane = lane_ids(z)
    per = LANES // (2 * PACK)
    for g in range(x // per):
        at = pl.ds(x // 2 * half + g * z, z)
        first, second = from1[at, :], from2[at, :]
        left = jnp.where(is_even, second, first)
        right = jnp.where(is_even, first, second)
        for j in range(per):
            i = g * per + j
            value = iterate[i]
            value = jnp.where((lane >= EDGE - PACK) & (lane < EDGE), lanes_roll(left, EDGE - PACK - 2 * PACK * j), value)
            value = jnp.where(
                (lane >= LANES - EDGE) & (lane < LANES - EDGE + PACK), lanes_roll(right, LANES - EDGE - PACK - 2 * PACK * j), value
            )
            wide[i] = value
            if i < HALO:
                head[pl.ds(x // 2 * half + i * z, z), :] = value
            if i >= x - HALO:
                tail[pl.ds(x // 2 * half + (i - x + HALO) * z, z), :] = value


def last_kernel(tiles, fine, one, two, iterate, restricted, before, after, before2, after2, win, w_before, w_after,
                e0, e1, e2, e3, v, u, v2, r2, spread, flux, water, frac):
    layer = lax.axis_index("layer")
    x, z = iterate.shape[0], iterate.shape[1]
    half = z // 2
    coarse_solve(one, two, right_rows(x, half, restricted, before, after, before2, after2), u, v2, r2, x)
    correct(u, v, x, spread, iterate, before, after)
    level = fine_level(fine, iterate)
    right = lambda i: fine[4, i]
    level.sweep(v, right, HALO - 5, HALO + x + 5)
    level.sweep(v, right, HALO - 4, HALO + x + 4)

    def cells(a, i):
        return halo_row(win, w_before, w_after, a, i, x, z)

    low, high = HALO - SUBSTEPS, HALO + x + SUBSTEPS
    for i in range(low, high):
        p = v[i]
        if i > low:
            flux[0, i] = fine[0, i] * (v[i - 1] - p)
        flux[1, i] = fine[1, i] * (p - lanes_roll(p, -1))
        flux[2, i] = fine[2, i] * (p - subs_roll(p, -1))
        water[i] = cells(4, i)
    for step in range(SUBSTEPS):
        for i in range(low + step, high - step):
            s = water[i]
            wetting = s * s
            frac[i] = wetting / (wetting + OIL_RATIO * (1.0 - s) * (1.0 - s))
        f = frac[low + step]
        g = flux[0, low + step + 1]
        above = frac[low + step + 1]
        inflow = g * jnp.where(g > 0.0, f, above)
        f = above
        for i in range(low + step + 1, high - step - 1):
            above = frac[i + 1]
            g = flux[0, i + 1]
            through = g * jnp.where(g > 0.0, f, above)
            gy = flux[1, i]
            through_y = gy * jnp.where(gy > 0.0, f, lanes_roll(f, -1))
            gz = flux[2, i]
            through_z = gz * jnp.where(gz > 0.0, f, subs_roll(f, -1))
            outflow = (through - inflow) + (through_y - lanes_roll(through_y, 1)) + (through_z - subs_roll(through_z, 1))
            wells = cells(6, i)
            water[i] = water[i] + STEP_RATE / cells(3, i) * (jnp.maximum(wells, 0.0) + f * jnp.minimum(wells, 0.0) - outflow)
            inflow, f = through, above
    lane = lane_ids(z)
    part = z // STRIPS
    outs = (e0, e1, e2, e3)
    for a, ref in enumerate((v, water)):
        for i in range(x // 2):
            first, second = ref[HALO + i], ref[HALO + x // 2 + i]
            pair = jnp.where(lane < LANES // 2, lanes_roll(first, -EDGE), lanes_roll(second, EDGE))
            ref[i] = pair

    def fill(me):
        for j in range(STRIPS):
            for a, ref in enumerate((v, water)):
                for i in range(x // 2):
                    outs[j][a, i] = ref[i, pl.ds((me ^ j) * part, part), :]

    for me in range(STRIPS):
        pl.when(layer == me)(functools.partial(fill, me))


def join_kernel(e0, e1, e2, e3, pressure, water):
    layer = lax.axis_index("layer")
    pieces = (e0, e1, e2, e3)
    x, part = pressure.shape[0], pressure.shape[1]
    lane = lane_ids(part)
    middle = LANES // 2

    def fill(me):
        strips = {strip_of(me ^ j): pieces[j] for j in range(STRIPS)}
        for a, out in enumerate((pressure, water)):
            for i in range(x // 2):
                for h in range(STRIPS // 2):
                    first, second = strips[2 * h][a, i], strips[2 * h + 1][a, i]
                    lanes = pl.ds(h * LANES, LANES)
                    out[i, :, lanes] = jnp.where(lane < middle, first, lanes_roll(second, middle))
                    out[i + x // 2, :, lanes] = jnp.where(lane < middle, lanes_roll(first, middle), second)

    for me in range(STRIPS):
        pl.when(layer == me)(functools.partial(fill, me))


def call(kernel, outs, scratch, *args, name):
    vmem = pl.BlockSpec(memory_space=pltpu.VMEM)
    shapes = [jax.ShapeDtypeStruct(s, jnp.float32) for s in outs]
    return pl.pallas_call(
        kernel,
        out_shape=shapes,
        in_specs=[vmem] * len(args),
        out_specs=[vmem] * len(outs),
        scratch_shapes=[pltpu.VMEM(s, jnp.float32) for s in scratch],
        compiler_params=pltpu.CompilerParams(vmem_limit_bytes=40 * 1024 * 1024),
        name=name,
    )(*args)


def along_layer(value, j):
    return lax.ppermute(value, "layer", [(i, i ^ j) for i in range(STRIPS)])


def along_tile(value, k):
    count = lax.axis_size("tile")
    return lax.ppermute(value, "tile", [(i, (i + k) % count) for i in range(count)])


def local(permeability, porosity, saturation, pressure_old, source):
    tiles = lax.axis_size("tile")
    x, part, _ = porosity.shape
    z = part * STRIPS
    half = z // 2
    rows = x + 2 * HALO
    chunk = (7, x, part, LANES)
    pieces = call(split_kernel, [chunk] * STRIPS, [], permeability, porosity, saturation, pressure_old, source, name="split")
    pieces = [pieces[0]] + [along_layer(pieces[j], j) for j in range(1, STRIPS)]

    c_rows = 4 * (x // 2) * half
    edge_rows = 7 * HALO * z + c_rows
    win, head, tail, c_here = call(
        window_kernel, [(7, x, z, LANES), (edge_rows, LANES), (edge_rows, LANES), (c_rows, LANES)], [(2 * x, z, LANES)], *pieces, name="window"
    )
    w_before, w_after = along_tile(tail, 1), along_tile(head, -1)
    c_before2, c_after2 = along_tile(c_here, 2), along_tile(c_here, -2)

    r_rows = x // 2 * half
    message_rows = r_rows + HALO * z
    fine, diag, iterate, restricted, head, tail = call(
        functools.partial(first_kernel, tiles),
        [(6, rows, z, LANES), (x, z, LANES), (x, z, LANES), (r_rows, LANES), (message_rows, LANES), (message_rows, LANES)],
        [(rows, z, LANES), (x // 2, z, LANES)],
        win, w_before, w_after, name="first",
    )
    before, after = along_tile(tail, 1), along_tile(head, -1)
    before2, after2 = along_tile(restricted, 2), along_tile(restricted, -2)

    rows1, rows2 = 5 * x // 2, 5 * x // 4
    solve_scratch = [(rows, z, LANES), (rows1, half, LANES), (rows2, half, LANES), (rows2, half, LANES), (rows // 2, z, LANES)]
    packed_rows = r_rows + x * 2 * PACK * z // LANES
    one, two, iterate, message = call(
        functools.partial(second_kernel, tiles),
        [(5, rows1, half, LANES), (5, rows2, half, LANES), (x, z, LANES), (packed_rows, LANES)],
        solve_scratch + [(x // 2, z, LANES)],
        fine, diag, iterate, restricted, before, after, before2, after2, c_here, w_before, w_after, c_before2, c_after2, name="second",
    )
    from1, from2 = along_layer(message, 1), along_layer(message, 2)
    iterate, restricted, head, tail = call(
        widen_kernel, [(x, z, LANES), (r_rows, LANES), (message_rows, LANES), (message_rows, LANES)], [],
        iterate, message, from1, from2, name="widen",
    )
    before, after = along_tile(tail, 1), along_tile(head, -1)
    before2, after2 = along_tile(restricted, 2), along_tile(restricted, -2)
    piece = (2, x // 2, part, LANES)
    pieces = call(
        functools.partial(last_kernel, tiles), [piece] * STRIPS,
        solve_scratch + [(3, rows, z, LANES), (rows, z, LANES), (rows, z, LANES)],
        fine, one, two, iterate, restricted, before, after, before2, after2, win, w_before, w_after, name="last",
    )
    pieces = [pieces[0]] + [along_layer(pieces[j], j) for j in range(1, STRIPS)]
    pressure, water = call(join_kernel, [porosity.shape, porosity.shape], [], *pieces, name="join")
    return pressure, water


def solution(mesh):
    return jax.shard_map(
        local,
        mesh=mesh,
        in_specs=(
            P(None, "tile", "layer", None),
            P("tile", "layer", None),
            P("tile", "layer", None),
            P("tile", "layer", None),
            P("tile", "layer", None),
        ),
        out_specs=(P("tile", "layer", None), P("tile", "layer", None)),
        check_vma=False,
    )
```
